512 devices in a mesh: blk: 64 (over x, y, z_hi, core), ulysses: 8 (over z_lo).
Axes of the slice: x: 4, y: 4, z: 16 (z_hi: 2, z_lo: 8; z = z_hi * 8 + z_lo), core: 2. Of those that a mesh axis runs over, the one named last changes fastest.
Arguments:
- query_rows: bfloat16 [8192, 3072], P('blk', 'ulysses'), may hold values from -8 to 8
- key_rows: bfloat16 [8192, 3072], P('blk', 'ulysses'), may hold values from -8 to 8
- value_rows: bfloat16 [8192, 3072], P('blk', 'ulysses'), may hold values from -6 to 6
Outputs:
- attended: bfloat16 [8192, 3072], P(('blk', 'ulysses'))
The draws below stay inside these ranges and needn't reach their ends.
All inputs are finite; a program needn't handle non-finite values.
Results may differ from the reference program's by a relative error of at most 0.0055.
Values may be sent and summed in bfloat16 or wider, within the bound.
A program may use at most 128 MiB of HBM per device.

```python
import math
import jax
import jax.numpy as jnp
from jax import lax

HEADS = 24
HD = 128
SEQ = 8192
TOKENS = 8192


def draw_query_rows(key, part):
    key = jax.random.fold_in(key, 3)
    drawn = jnp.clip(1.7 * jax.random.normal(key, (TOKENS, HEADS * HD), jnp.float32), -8.0, 8.0)
    return drawn.astype(jnp.bfloat16)


def draw_key_rows(key, part):
    key = jax.random.fold_in(key, 4)
    drawn = jnp.clip(1.7 * jax.random.normal(key, (TOKENS, HEADS * HD), jnp.float32), -8.0, 8.0)
    return drawn.astype(jnp.bfloat16)


def block_levels(rng, shape, split, low, largest):
    def one(axis_at, parts):
        draws = jax.random.uniform(jax.random.fold_in(jax.random.fold_in(rng, 6), axis_at), (parts,), jnp.float32, low / len(split), largest / len(split))
        return jnp.repeat(jnp.exp(draws), shape[axis_at] // parts).reshape((-1,) + (1,) * (len(shape) - axis_at - 1))

    loudness = one(*split[0])
    for cut in split[1:]:
        loudness = loudness * one(*cut)
    return loudness


def bell_draw(stream_key, dims, deviation, limit, cuts=(), kind=jnp.bfloat16):
    result = deviation * jax.random.normal(stream_key, dims, jnp.float32)
    if cuts:
        result = result * block_levels(stream_key, dims, cuts, -0.22, 0.18)
    return jnp.clip(result, -limit, limit).astype(kind)


def setup_inputs(seed: int = 0) -> dict:
    arg_keys = jax.random.split(jax.random.key(seed), 4)
    return {
        "query_rows": draw_query_rows(jax.random.fold_in(arg_keys[3], 71), 0),
        "key_rows": draw_key_rows(jax.random.fold_in(arg_keys[3], 71), 0),
        "value_rows": bell_draw(arg_keys[2], (TOKENS, HEADS * HD), 1.0, 6.0, ((0, 64), (1, 8))),
    }


def one_head(query_head, key_head, value_head):
    rows_block = math.gcd(SEQ, 512)
    query_blocks = query_head.reshape(SEQ // rows_block, rows_block, HD)

    def attend(query_block):
        scores = jnp.dot(query_block, key_head.T, preferred_element_type=jnp.float32) * (HD ** -0.5)
        row_peak = jnp.max(scores, axis=1, keepdims=True)
        raised = jnp.exp(scores - row_peak)
        totals = jnp.sum(raised, axis=1, keepdims=True)
        weights = raised.astype(jnp.bfloat16)
        summed = jnp.dot(weights, value_head, preferred_element_type=jnp.float32)
        return (summed / totals).astype(jnp.bfloat16)

    return lax.map(attend, query_blocks).reshape(SEQ, HD)


def to_heads(matrix):
    return matrix.reshape(SEQ, HEADS, HD).transpose(1, 0, 2)


def head_task(triple):
    return one_head(triple[0], triple[1], triple[2])


def reference(query_rows, key_rows, value_rows):
    attended = lax.map(head_task, (to_heads(query_rows), to_heads(key_rows), to_heads(value_rows)))
    return attended.transpose(1, 0, 2).reshape(TOKENS, HEADS * HD)
```

```python
import functools

import jax
import jax.numpy as jnp
from jax import lax
from jax.experimental import pallas as pl
from jax.experimental.pallas import tpu as pltpu
from jax.sharding import PartitionSpec as P

HD = 128
ROWS = 128
HALF = 64
OUT_ROWS = 16
MESH = pl.DeviceIdType.MESH
FACTOR = HD**-0.5 * 1.4426950408889634
F32 = jnp.float32
BF16 = jnp.bfloat16


def role(z):
    return 1 - lax.rem((z + 4) // 8, 2)


def soft_tile(keys_at, values_at, q, scores):
    peak = jnp.full((8, q.shape[0]), -jnp.inf, F32)
    for j in range(8):
        s = lax.dot_general(keys_at(j), q, (((1,), (1,)), ((), ())), preferred_element_type=F32)
        scores[j] = s
        peak = jnp.maximum(peak, jnp.max(s.reshape(32, 8, -1), axis=0))
    peak = jnp.max(peak, axis=0, keepdims=True)
    total = jnp.zeros((8, q.shape[0]), F32)
    sums = jnp.zeros((HD, q.shape[0]), F32)
    for j in range(8):
        p = jnp.exp2((scores[j] - peak) * FACTOR)
        total = total + jnp.sum(p.reshape(32, 8, -1), axis=0)
        sums = sums + jnp.dot(values_at(j), p.astype(BF16), preferred_element_type=F32)
    total = jnp.sum(total, axis=0, keepdims=True)
    return sums, peak, total


def pack(ref, at, sums, peak, total):
    ref[at, :HD] = sums
    ref[at, HD:] = jnp.concatenate([peak, total, jnp.zeros((6, peak.shape[1]), F32)], axis=0)


def merge(parts):
    peaks = [p[HD : HD + 1] for p in parts]
    top = functools.reduce(jnp.maximum, peaks)
    fades = [jnp.exp2((peak - top) * FACTOR) for peak in peaks]
    total = sum(p[HD + 1 : HD + 2] * f for p, f in zip(parts, fades))
    sums = sum(p[:HD] * f for p, f in zip(parts, fades))
    return (sums / total).T.astype(BF16)


def kernel(
    q_ref, k_ref, v_ref, o_ref,
    full, mid, full_q, mid_q, full_vt, mid_vt, scores,
    full_part, mid_part, full_got, mid_got, full_out, mid_out, landed,
    z_s, z_r, y_s, y_r, c_s, c_r, x_s, x_r, p_s, p_r, o_s, o_r,
):
    b = lax.axis_index("blk")
    zl = lax.axis_index("ulysses")
    c = lax.rem(b, 2)
    z = lax.rem(b // 2, 2) * 8 + zl
    y = lax.rem(b // 4, 4)
    x = b // 16

    def at(dx=0, dy=0, dz=0, dc=0):
        tx, ty = lax.rem(x + dx, 4), lax.rem(y + dy, 4)
        tz, tc = lax.rem(z + dz, 16), lax.rem(c + dc, 2)
        return (((tx * 4 + ty) * 2 + tz // 8) * 2 + tc, lax.rem(tz, 8))

    def copy(src, dst, s_sem, r_sem, where):
        return pltpu.make_async_remote_copy(
            src_ref=src, dst_ref=dst, send_sem=s_sem, recv_sem=r_sem, device_id=where, device_id_type=MESH
        )

    sent = []

    def send(*args):
        one = copy(*args)
        one.start()
        sent.append(one)

    barrier = pltpu.get_barrier_semaphore()
    peers = [at(dz=d) for d in range(1, 16)]
    peers += [at(dy=d) for d in range(1, 4)] + [at(dx=d) for d in range(1, 4)] + [at(dc=1)]
    for peer in peers:
        pl.semaphore_signal(barrier, inc=1, device_id=peer, device_id_type=MESH)
    pl.semaphore_wait(barrier, len(peers))

    mine = c * 4 + y
    here = at()
    holders = ((full, full_q, ROWS), (mid, mid_q, HALF))

    def z_dst(item, s):
        held, held_q, rows = holders[item // 3]
        if item % 3 == 0:
            return held_q.at[x, pl.ds(s * rows, rows)]
        return held.at[item % 3 - 1, mine, pl.ds(s * ROWS, ROWS)]

    for item in range(6):
        for s, dz in ((0, 4), (1, 12)):
            r = role(lax.rem(z + dz, 16))
            ref = (q_ref, k_ref, v_ref)[item % 3]
            if item < 3:
                src = ref.at[:, pl.ds(pl.multiple_of(r * 256, 128), HD)]
            elif item == 3:
                src = ref.at[pl.ds(pl.multiple_of(r * HALF, HALF), HALF), pl.ds(HD, HD)]
            else:
                src = ref.at[:, pl.ds(HD, HD)]
            send(src, z_dst(item, s), z_s.at[item, s], z_r.at[item, s], at(dz=dz))

    def z_wait(item, s):
        dst = z_dst(item, s)
        copy(dst, dst, z_s.at[item, s], z_r.at[item, s], here).wait_recv()

    def spread_queries(head):
        held_q, rows = holders[head][1:]
        for s in range(2):
            z_wait(head * 3, s)
            for dx in range(1, 4):
                part = held_q.at[x, pl.ds(s * rows, rows)]
                send(part, part, x_s.at[head, s, dx - 1], x_r.at[head, s, dx - 1], at(dx=dx))

    def wait_queries(head):
        held_q, rows = holders[head][1:]
        for s in range(2):
            for dx in range(1, 4):
                part = held_q.at[lax.rem(x - dx + 4, 4), pl.ds(s * rows, rows)]
                copy(part, part, x_s.at[head, s, dx - 1], x_r.at[head, s, dx - 1], here).wait_recv()

    def pass_on(head, kv, dy):
        held = holders[head][0]
        part = held.at[kv, c * 4 + lax.rem(y - dy + 4, 4)]
        send(part, part, c_s.at[head, kv, dy], c_r.at[head, kv, dy], at(dc=1))

    def spread_block(head, kv):
        held = holders[head][0]
        for s in range(2):
            z_wait(head * 3 + 1 + kv, s)
            for dy in range(1, 4):
                part = held.at[kv, mine, pl.ds(s * ROWS, ROWS)]
                send(part, part, y_s.at[head, kv, s, dy - 1], y_r.at[head, kv, s, dy - 1], at(dy=dy))
        pass_on(head, kv, 0)

    def relay_block(head, kv):
        held = holders[head][0]
        for dy in range(1, 4):
            for s in range(2):
                part = held.at[kv, c * 4 + lax.rem(y - dy + 4, 4), pl.ds(s * ROWS, ROWS)]
                copy(part, part, y_s.at[head, kv, s, dy - 1], y_r.at[head, kv, s, dy - 1], here).wait_recv()
            pass_on(head, kv, dy)

    def wait_block(head, kv):
        held = holders[head][0]
        for dy in range(4):
            part = held.at[kv, (1 - c) * 4 + lax.rem(y - dy + 4, 4)]
            copy(part, part, c_s.at[head, kv, dy], c_r.at[head, kv, dy], here).wait_recv()

    def turn_values(head, turned):
        held = holders[head][0]
        for j in range(8):
            turned[j] = held[1, j].T

    def send_part(head, dx):
        part, got = ((full_part, full_got), (mid_part, mid_got))[head]
        send(part.at[dx], got.at[dx - 1], p_s.at[head, dx - 1], p_r.at[head, dx - 1], at(dx=dx))

    def full_tile(dx):
        q = full_q[lax.rem(x + dx, 4)]
        pack(full_part, dx, *soft_tile(lambda j: full[0, j], lambda j: full_vt[j], q, scores))
        if dx:
            send_part(0, dx)

    def mid_tile(dx_a, dx_b):
        q = jnp.concatenate([mid_q[lax.rem(x + dx_a, 4)], mid_q[lax.rem(x + dx_b, 4)]], axis=0)
        sums, peak, total = soft_tile(lambda j: mid[0, j], lambda j: mid_vt[j], q, scores)
        for i, dx in enumerate((dx_a, dx_b)):
            cut = slice(i * ROWS, (i + 1) * ROWS)
            pack(mid_part, dx, sums[:, cut], peak[:, cut], total[:, cut])
            if dx:
                send_part(1, dx)

    def wait_parts(head):
        got = (full_got, mid_got)[head]
        for dx in range(1, 4):
            copy(got.at[dx - 1], got.at[dx - 1], p_s.at[head, dx - 1], p_r.at[head, dx - 1], here).wait_recv()

    spread_queries(0)
    spread_block(0, 0)
    spread_block(0, 1)
    relay_block(0, 0)
    spread_queries(1)
    relay_block(0, 1)
    wait_queries(0)
    wait_block(0, 0)
    wait_block(0, 1)
    turn_values(0, full_vt)
    full_tile(2)
    spread_block(1, 0)
    full_tile(1)
    full_tile(3)
    spread_block(1, 1)
    full_tile(0)
    relay_block(1, 0)
    relay_block(1, 1)
    wait_queries(1)
    wait_block(1, 0)
    wait_block(1, 1)
    turn_values(1, mid_vt)
    mid_tile(2, 1)
    mid_tile(3, 0)

    r = role(z)
    first = lax.rem(z + 12, 16) // 8
    head_base = lax.rem(z + 4, 8) * 3

    def hand_over(out, row, head, tz, sem):
        src = out.at[pl.ds(pl.multiple_of(row, OUT_ROWS), OUT_ROWS)]
        dst = landed.at[:, pl.ds(pl.multiple_of(head * HD, HD), HD)]
        return src, dst, sem, o_r, (((x * 4 + y) * 2 + tz // 8) * 2 + c, lax.rem(tz, 8))

    wait_parts(0)
    full_out[...] = merge([full_part[0]] + [full_got[i] for i in range(3)])
    for d in range(16):
        tz = lax.rem(z + d, 16)
        s = lax.rem(first + tz // 8, 2)
        move = hand_over(full_out, s * ROWS + lax.rem(tz, 8) * OUT_ROWS, head_base + 2 * r, tz, o_s.at[d])
        if d:
            send(*move)
        else:
            pltpu.make_async_copy(move[0], move[1], o_r).start()

    wait_parts(1)
    mid_out[...] = merge([mid_part[0]] + [mid_got[i] for i in range(3)])
    late = []
    for half in range(2):
        for i in range(4):
            tz = half * 8 + 4 * r + i
            s = lax.rem(first + half, 2)
            move = hand_over(mid_out, s * HALF + i * OUT_ROWS, head_base + 1, tz, o_s.at[16 + half * 4 + i])
            one = copy(*move)
            late.append((tz, one))

            @pl.when(tz != z)
            def _():
                one.start()

            @pl.when(tz == z)
            def _():
                pltpu.make_async_copy(move[0], move[1], o_r).start()

    pltpu.make_async_copy(landed, landed, o_r).wait()
    o_ref[...] = landed[...]
    for one in sent:
        one.wait_send()
    for tz, one in late:

        @pl.when(tz != z)
        def _():
            one.wait_send()


def on_device(query_rows, key_rows, value_rows):
    dma = pltpu.SemaphoreType.DMA
    return pl.pallas_call(
        kernel,
        out_shape=jax.ShapeDtypeStruct((OUT_ROWS, 24 * HD), BF16),
        in_specs=[pl.BlockSpec(memory_space=pl.ANY)] * 3,
        out_specs=pl.BlockSpec(memory_space=pltpu.VMEM),
        scratch_shapes=[
            pltpu.VMEM((2, 8, 256, HD), BF16),
            pltpu.VMEM((2, 8, 256, HD), BF16),
            pltpu.VMEM((4, 256, HD), BF16),
            pltpu.VMEM((4, 128, HD), BF16),
            pltpu.VMEM((8, HD, 256), BF16),
            pltpu.VMEM((8, HD, 256), BF16),
            pltpu.VMEM((8, 256, 256), F32),
            pltpu.VMEM((4, HD + 8, 256), F32),
            pltpu.VMEM((4, HD + 8, 128), F32),
            pltpu.VMEM((3, HD + 8, 256), F32),
            pltpu.VMEM((3, HD + 8, 128), F32),
            pltpu.VMEM((256, HD), BF16),
            pltpu.VMEM((128, HD), BF16),
            pltpu.VMEM((OUT_ROWS, 24 * HD), BF16),
            dma((6, 2)), dma((6, 2)),
            dma((2, 2, 2, 3)), dma((2, 2, 2, 3)),
            dma((2, 2, 4)), dma((2, 2, 4)),
            dma((2, 2, 3)), dma((2, 2, 3)),
            dma((2, 3)), dma((2, 3)),
            dma((24,)), dma(()),
        ],
        compiler_params=pltpu.CompilerParams(
            collective_id=0, has_side_effects=True, vmem_limit_bytes=40 * 2**20
        ),
        name="attend",
    )(query_rows, key_rows, value_rows)


def solution(mesh):
    return jax.shard_map(
        on_device,
        mesh=mesh,
        in_specs=(P("blk", "ulysses"), P("blk", "ulysses"), P("blk", "ulysses")),
        out_specs=P(("blk", "ulysses"), None),
        check_vma=False,
    )
```

```python
import functools

import jax
import jax.numpy as jnp
from jax import lax
from jax.experimental import pallas as pl
from jax.experimental.pallas import tpu as pltpu
from jax.sharding import PartitionSpec as P

HD = 128
ROWS = 128
HALF = 64
OUT_ROWS = 16
MESH = pl.DeviceIdType.MESH
FACTOR = HD**-0.5 * 1.4426950408889634
F32 = jnp.float32
BF16 = jnp.bfloat16


def role(z):
    return 1 - lax.rem((z + 4) // 8, 2)


def weigh_tile(keys_at, q, scores, weights):
    peak = jnp.full((8, q.shape[0]), -jnp.inf, F32)
    for j in range(8):
        s = lax.dot_general(keys_at(j), q, (((1,), (1,)), ((), ())), preferred_element_type=F32)
        scores[j] = s
        peak = jnp.maximum(peak, jnp.max(s.reshape(32, 8, -1), axis=0))
    peak = jnp.max(peak, axis=0, keepdims=True)
    total = jnp.zeros((8, q.shape[0]), F32)
    for j in range(8):
        p = jnp.exp2((scores[j] - peak) * FACTOR)
        total = total + jnp.sum(p.reshape(32, 8, -1), axis=0)
        weights[j] = p.astype(BF16)
    return peak, jnp.sum(total, axis=0, keepdims=True)


def sum_tile(values_at, weights):
    return sum(jnp.dot(values_at(j), weights[j], preferred_element_type=F32) for j in range(8))


def pack(ref, at, sums, peak, total):
    ref[at, :HD] = sums
    ref[at, HD:] = jnp.concatenate([peak, total, jnp.zeros((6, peak.shape[1]), F32)], axis=0)


def merge(parts):
    peaks = [p[HD : HD + 1] for p in parts]
    top = functools.reduce(jnp.maximum, peaks)
    fades = [jnp.exp2((peak - top) * FACTOR) for peak in peaks]
    total = sum(p[HD + 1 : HD + 2] * f for p, f in zip(parts, fades))
    sums = sum(p[:HD] * f for p, f in zip(parts, fades))
    return (sums / total).T.astype(BF16)


def kernel(
    q_ref, k_ref, v_ref, o_ref,
    full, mid, full_q, mid_q, full_vt, mid_vt, scores, weights,
    full_part, mid_part, full_got, mid_got, full_out, mid_out, landed,
    z_s, z_r, y_s, y_r, c_s, c_r, x_s, x_r, p_s, p_r, o_s, o_r,
):
    b = lax.axis_index("blk")
    zl = lax.axis_index("ulysses")
    c = lax.rem(b, 2)
    z = lax.rem(b // 2, 2) * 8 + zl
    y = lax.rem(b // 4, 4)
    x = b // 16

    def at(dx=0, dy=0, dz=0, dc=0):
        tx, ty = lax.rem(x + dx, 4), lax.rem(y + dy, 4)
        tz, tc = lax.rem(z + dz, 16), lax.rem(c + dc, 2)
        return (((tx * 4 + ty) * 2 + tz // 8) * 2 + tc, lax.rem(tz, 8))

    def copy(src, dst, s_sem, r_sem, where):
        return pltpu.make_async_remote_copy(
            src_ref=src, dst_ref=dst, send_sem=s_sem, recv_sem=r_sem, device_id=where, device_id_type=MESH
        )

    def send(*args):
        copy(*args).start()

    def landed_all(ref, sem):
        pltpu.make_async_copy(ref, ref, sem).wait()

    barrier = pltpu.get_barrier_semaphore()
    peers = [at(dz=d) for d in (1, 2, 4, 12, 14, 15)]
    peers += [at(dy=d) for d in range(1, 4)] + [at(dx=d) for d in range(1, 4)] + [at(dc=1)]
    for peer in peers:
        pl.semaphore_signal(barrier, inc=1, device_id=peer, device_id_type=MESH)
    pl.semaphore_wait(barrier, len(peers))

    holders = ((full, full_q, ROWS), (mid, mid_q, HALF))
    block_at, query_at = (y, y), (x, x)

    def along_blocks(head, d):
        return at(dy=d)

    def along_queries(head, d):
        return at(dx=d)

    def block_from(head, d):
        return c * 4 + lax.rem(block_at[head] - d + 4, 4)

    def z_start(head, item):
        held, held_q, rows = holders[head]
        for s, dz in ((0, 4), (1, 12)):
            r = role(lax.rem(z + dz, 16))
            ref = (k_ref, v_ref, q_ref)[item]
            if head == 0:
                src = ref.at[:, pl.ds(pl.multiple_of(r * 256, 128), HD)]
            elif item == 2:
                src = ref.at[pl.ds(pl.multiple_of(r * HALF, HALF), HALF), pl.ds(HD, HD)]
            else:
                src = ref.at[:, pl.ds(HD, HD)]
            if item == 2:
                dst = held_q.at[query_at[head], pl.ds(s * rows, rows)]
            else:
                dst = held.at[item, block_from(head, 0), pl.ds(s * ROWS, ROWS)]
            send(src, dst, z_s.at[head, item], z_r.at[head, item], at(dz=dz))

    def z_sent(head, item):
        held, held_q, rows = holders[head]
        landed_all(held_q.at[0] if item == 2 else held.at[item, 0], z_s.at[head, item])

    def z_wait(head, item):
        held, held_q, rows = holders[head]
        landed_all(held_q.at[query_at[head]] if item == 2 else held.at[item, block_from(head, 0)], z_r.at[head, item])

    def spread_queries(head):
        held_q = holders[head][1]
        z_wait(head, 2)
        part = held_q.at[query_at[head]]
        for d in range(1, 4):
            send(part, part, x_s, x_r.at[head], along_queries(head, d))

    def wait_queries(head):
        held_q = holders[head][1]
        landed_all(held_q.at[pl.ds(0, 3)], x_r.at[head])

    def pass_on(head, kv, d):
        part = holders[head][0].at[kv, block_from(head, d)]
        send(part, part, c_s, c_r.at[head, kv], at(dc=1))

    def spread_block(head, kv):
        part = holders[head][0].at[kv, block_from(head, 0)]
        z_wait(head, kv)
        for d in range(1, 4):
            send(part, part, y_s, y_r.at[head, kv, d - 1], along_blocks(head, d))
        pass_on(head, kv, 0)

    def relay_block(head, kv):
        for d in range(1, 4):
            landed_all(holders[head][0].at[kv, block_from(head, d)], y_r.at[head, kv, d - 1])
            pass_on(head, kv, d)

    def wait_block(head, kv):
        landed_all(holders[head][0].at[kv, pl.ds((1 - c) * 4, 4)], c_r.at[head, kv])

    def turn_values(head, turned):
        held = holders[head][0]
        for j in range(8):
            turned[j] = held[1, j].T

    def send_part(head, d):
        part, got = ((full_part, full_got), (mid_part, mid_got))[head]
        send(part.at[d], got.at[d - 1], p_s.at[head], p_r.at[head], along_queries(head, d))

    def full_tile(d):
        q = full_q[lax.rem(query_at[0] + d, 4)]
        peak, total = weigh_tile(lambda j: full[0, j], q, scores, weights.at[0])
        pack(full_part, d, sum_tile(lambda j: full_vt[j], weights.at[0]), peak, total)
        if d:
            send_part(0, d)

    def mid_weigh(i, d_a, d_b):
        q = jnp.concatenate([mid_q[lax.rem(query_at[1] + d, 4)] for d in (d_a, d_b)], axis=0)
        return weigh_tile(lambda j: mid[0, j], q, scores, weights.at[i])

    def mid_sum(i, d_a, d_b, peak, total):
        sums = sum_tile(lambda j: mid_vt[j], weights.at[i])
        for k, d in enumerate((d_a, d_b)):
            cut = slice(k * ROWS, (k + 1) * ROWS)
            pack(mid_part, d, sums[:, cut], peak[:, cut], total[:, cut])
            if d:
                send_part(1, d)

    z_start(0, 0)
    z_start(0, 1)
    z_sent(0, 0)
    z_sent(0, 1)
    z_start(1, 0)
    z_start(0, 2)
    spread_block(0, 0)
    spread_block(0, 1)
    z_sent(1, 0)
    z_sent(0, 2)
    z_start(1, 1)
    z_start(1, 2)
    relay_block(0, 0)
    spread_block(1, 0)
    spread_queries(0)
    relay_block(0, 1)
    spread_block(1, 1)
    spread_queries(1)
    relay_block(1, 0)
    wait_block(0, 0)
    wait_block(0, 1)
    turn_values(0, full_vt)
    wait_queries(0)
    full_tile(2)
    full_tile(1)
    relay_block(1, 1)
    full_tile(3)
    full_tile(0)
    wait_block(1, 0)
    wait_queries(1)
    first_pair = mid_weigh(0, 2, 1)
    other_pair = mid_weigh(1, 3, 0)
    wait_block(1, 1)
    turn_values(1, mid_vt)
    mid_sum(0, 2, 1, *first_pair)
    mid_sum(1, 3, 0, *other_pair)
    z_sent(1, 1)
    z_sent(1, 2)

    r = role(z)
    first = lax.rem(z + 12, 16) // 8
    head_base = lax.rem(z + 4, 8) * 3

    def hand_over(out, row, head, tz, sem):
        src = out.at[pl.ds(pl.multiple_of(row, OUT_ROWS), OUT_ROWS)]
        dst = landed.at[:, pl.ds(pl.multiple_of(head * HD, HD), HD)]
        return src, dst, sem, o_r, (((x * 4 + y) * 2 + tz // 8) * 2 + c, lax.rem(tz, 8))

    landed_all(full_got, p_r.at[0])
    full_out[...] = merge([full_part[0]] + [full_got[i] for i in range(3)])
    for d in range(16):
        tz = lax.rem(z + d, 16)
        s = lax.rem(first + tz // 8, 2)
        move = hand_over(full_out, s * ROWS + lax.rem(tz, 8) * OUT_ROWS, head_base + 2 * r, tz, o_s.at[0])
        if d:
            send(*move)
        else:
            pltpu.make_async_copy(move[0], move[1], o_r).start()

    landed_all(mid_got, p_r.at[1])
    mid_out[...] = merge([mid_part[0]] + [mid_got[i] for i in range(3)])
    for half in range(2):
        for i in range(4):
            tz = half * 8 + 4 * r + i
            s = lax.rem(first + half, 2)
            move = hand_over(mid_out, s * HALF + i * OUT_ROWS, head_base + 1, tz, o_s.at[1])

            @pl.when(tz != z)
            def _():
                send(*move)

            @pl.when(tz == z)
            def _():
                pltpu.make_async_copy(move[0], move[1], o_r).start()

    landed_all(landed, o_r)
    o_ref[...] = landed[...]
    landed_all(full.at[:, pl.ds(0, 6)], y_s)
    landed_all(full, c_s)
    landed_all(full.at[0, :, pl.ds(0, 144)], x_s)
    landed_all(full_got, p_s.at[0])
    landed_all(mid_got, p_s.at[1])
    landed_all(landed.at[:, pl.ds(0, 15 * HD)], o_s.at[0])

    @pl.when(z < 8)
    def _():
        landed_all(landed.at[:, pl.ds(0, 8 * HD)], o_s.at[1])

    @pl.when(z >= 8)
    def _():
        landed_all(landed.at[:, pl.ds(0, 7 * HD)], o_s.at[1])


def on_device(query_rows, key_rows, value_rows):
    dma = pltpu.SemaphoreType.DMA
    return pl.pallas_call(
        kernel,
        out_shape=jax.ShapeDtypeStruct((OUT_ROWS, 24 * HD), BF16),
        in_specs=[pl.BlockSpec(memory_space=pl.ANY)] * 3,
        out_specs=pl.BlockSpec(memory_space=pltpu.VMEM),
        scratch_shapes=[
            pltpu.VMEM((2, 8, 256, HD), BF16),
            pltpu.VMEM((2, 8, 256, HD), BF16),
            pltpu.VMEM((4, 256, HD), BF16),
            pltpu.VMEM((4, 128, HD), BF16),
            pltpu.VMEM((8, HD, 256), BF16),
            pltpu.VMEM((8, HD, 256), BF16),
            pltpu.VMEM((8, 256, 256), F32),
            pltpu.VMEM((2, 8, 256, 256), BF16),
            pltpu.VMEM((4, HD + 8, 256), F32),
            pltpu.VMEM((4, HD + 8, 128), F32),
            pltpu.VMEM((3, HD + 8, 256), F32),
            pltpu.VMEM((3, HD + 8, 128), F32),
            pltpu.VMEM((256, HD), BF16),
            pltpu.VMEM((128, HD), BF16),
            pltpu.VMEM((OUT_ROWS, 24 * HD), BF16),
            dma((2, 3)), dma((2, 3)),
            dma(()), dma((2, 2, 3)),
            dma(()), dma((2, 2)),
            dma(()), dma((2,)),
            dma((2,)), dma((2,)),
            dma((2,)), dma(()),
        ],
        compiler_params=pltpu.CompilerParams(
            collective_id=0, has_side_effects=True, vmem_limit_bytes=60 * 2**20
        ),
        name="attend",
    )(query_rows, key_rows, value_rows)


def solution(mesh):
    return jax.shard_map(
        on_device,
        mesh=mesh,
        in_specs=(P("blk", "ulysses"), P("blk", "ulysses"), P("blk", "ulysses")),
        out_specs=P(("blk", "ulysses"), None),
        check_vma=False,
    )
```

```python
import functools

import jax
import jax.numpy as jnp
from jax import lax
from jax.experimental import pallas as pl
from jax.experimental.pallas import tpu as pltpu
from jax.sharding import PartitionSpec as P

HD = 128
ROWS = 128
OUT_ROWS = 16
MESH = pl.DeviceIdType.MESH
FACTOR = HD**-0.5 * 1.4426950408889634
F32 = jnp.float32
BF16 = jnp.bfloat16


def role(z):
    return 1 - lax.rem((z + 4) // 8, 2)


def weigh_tile(keys_at, q, scores, weights):
    peak = jnp.full((8, q.shape[0]), -jnp.inf, F32)
    for j in range(8):
        s = lax.dot_general(keys_at(j), q, (((1,), (1,)), ((), ())), preferred_element_type=F32)
        scores[j] = s
        peak = jnp.maximum(peak, jnp.max(s.reshape(32, 8, -1), axis=0))
    peak = jnp.max(peak, axis=0, keepdims=True)
    total = jnp.zeros((8, q.shape[0]), F32)
    for j in range(8):
        p = jnp.exp2((scores[j] - peak) * FACTOR)
        total = total + jnp.sum(p.reshape(32, 8, -1), axis=0)
        weights[j] = p.astype(BF16)
    return peak, jnp.sum(total, axis=0, keepdims=True)


def sum_tile(values_at, weights):
    return sum(jnp.dot(values_at(j), weights[j], preferred_element_type=F32) for j in range(8))


def pack(ref, at, sums, peak, total):
    ref[at, :HD] = sums
    ref[at, HD:] = jnp.concatenate([peak, total, jnp.zeros((6, peak.shape[1]), F32)], axis=0)


def merge(parts):
    peaks = [p[HD : HD + 1] for p in parts]
    top = functools.reduce(jnp.maximum, peaks)
    fades = [jnp.exp2((peak - top) * FACTOR) for peak in peaks]
    total = sum(p[HD + 1 : HD + 2] * f for p, f in zip(parts, fades))
    sums = sum(p[:HD] * f for p, f in zip(parts, fades))
    return (sums / total).T.astype(BF16)


def kernel(
    q_ref, k_ref, v_ref, o_ref,
    full, mid, full_q, mid_q, full_vt, mid_vt, scores, weights,
    full_part, mid_part, full_got, mid_got, full_out, mid_out, landed,
    z_s, z_r, y_s, y_r, c_s, c_r, x_s, x_r, p_s, p_r, o_s, o_r, l_s,
):
    b = lax.axis_index("blk")
    zl = lax.axis_index("ulysses")
    c = lax.rem(b, 2)
    z = lax.rem(b // 2, 2) * 8 + zl
    y = lax.rem(b // 4, 4)
    x = b // 16

    def at(dx=0, dy=0, dz=0, dc=0):
        tx, ty = lax.rem(x + dx, 4), lax.rem(y + dy, 4)
        tz, tc = lax.rem(z + dz, 16), lax.rem(c + dc, 2)
        return (((tx * 4 + ty) * 2 + tz // 8) * 2 + tc, lax.rem(tz, 8))

    def copy(src, dst, s_sem, r_sem, where):
        return pltpu.make_async_remote_copy(
            src_ref=src, dst_ref=dst, send_sem=s_sem, recv_sem=r_sem, device_id=where, device_id_type=MESH
        )

    def send(*args):
        copy(*args).start()

    def landed_all(ref, sem):
        pltpu.make_async_copy(ref, ref, sem).wait()

    barrier = pltpu.get_barrier_semaphore()
    peers = [at(dz=d) for d in (1, 2, 4, 12, 14, 15)]
    peers += [at(dy=d) for d in range(1, 4)] + [at(dx=d) for d in range(1, 4)] + [at(dc=1)]
    for peer in peers:
        pl.semaphore_signal(barrier, inc=1, device_id=peer, device_id_type=MESH)
    pl.semaphore_wait(barrier, len(peers))

    held_by, queries_by = (full, mid), (full_q, mid_q)
    columns = pl.ds(HD, HD)

    def block(head, kv, d, s=None):
        ref = held_by[head].at[kv, c * 4 + lax.rem(y - d + 4, 4)]
        return ref if s is None else ref.at[pl.ds(s * ROWS, ROWS)]

    def z_start(item):
        for s, dz in ((0, 4), (1, 12)):
            r = role(lax.rem(z + dz, 16))
            src = (k_ref, v_ref, q_ref)[item].at[:, pl.ds(pl.multiple_of(r * 256, 128), HD)]
            dst = full_q.at[x, pl.ds(s * ROWS, ROWS)] if item == 2 else block(0, item, 0, s)
            send(src, dst, z_s.at[item], z_r.at[item], at(dz=dz))

    def z_ref(item):
        return full_q.at[x] if item == 2 else block(0, item, 0)

    def z_sent(item):
        landed_all(z_ref(item), z_s.at[item])

    def m_start(kv):
        src = (k_ref, v_ref)[kv].at[:, columns]
        send(src, block(1, kv, 0, 1), z_s.at[3 + kv], z_r.at[3 + kv], at(dz=8))

    def m_sent(kv):
        landed_all(block(1, kv, 0, 1), z_s.at[3 + kv])

    def own_queries():
        src, dst = q_ref.at[:, columns], mid_q.at[x]
        for d in range(1, 4):
            send(src, dst, x_s, x_r.at[1], at(dx=d))
        pltpu.make_async_copy(src, dst, l_s).start()

    def own_block(kv):
        src, dst = (k_ref, v_ref)[kv].at[:, columns], block(1, kv, 0, 0)
        for d in range(1, 4):
            send(src, dst, y_s, y_r.at[2 + kv, d - 1], at(dy=d))
        send(src, dst, c_s, c_r.at[2 + kv], at(dc=1))
        pltpu.make_async_copy(src, dst, l_s).start()

    def own_landed():
        landed_all(mid.at[0, pl.ds(0, 3), pl.ds(0, ROWS)], l_s)

    def spread_queries():
        landed_all(z_ref(2), z_r.at[2])
        for d in range(1, 4):
            send(full_q.at[x], full_q.at[x], x_s, x_r.at[0], at(dx=d))

    def wait_queries(head):
        landed_all(queries_by[head].at[pl.ds(0, 3)], x_r.at[head])

    def kind_block(kind, d):
        return block(0, kind, d) if kind < 2 else block(1, kind % 2, d, kind // 2 - 1)

    def pass_on(kind, d):
        part = kind_block(kind, d)
        send(part, part, c_s, c_r.at[kind], at(dc=1))

    def spread_block(kind):
        part = kind_block(kind, 0)
        landed_all(part, z_r.at[kind if kind < 2 else kind - 1])
        for d in range(1, 4):
            send(part, part, y_s, y_r.at[kind, d - 1], at(dy=d))
        pass_on(kind, 0)

    def relay_block(kind):
        for d in range(1, 4):
            landed_all(kind_block(kind, d), y_r.at[kind, d - 1])
            pass_on(kind, d)

    def wait_block(kind):
        other = pl.ds((1 - c) * 4, 4)
        if kind < 2:
            landed_all(full.at[kind, other], c_r.at[kind])
        else:
            landed_all(mid.at[kind % 2, other, pl.ds((kind // 2 - 1) * ROWS, ROWS)], c_r.at[kind])

    def turn_values(head, turned):
        for j in range(8):
            turned[j] = held_by[head][1, j].T

    def send_part(head, d):
        part, got = ((full_part, full_got), (mid_part, mid_got))[head]
        send(part.at[d], got.at[d - 1], p_s.at[head], p_r.at[head], at(dx=d))

    def full_tile(d):
        q = full_q[lax.rem(x + d, 4)]
        peak, total = weigh_tile(lambda j: full[0, j], q, scores, weights.at[0])
        pack(full_part, d, sum_tile(lambda j: full_vt[j], weights.at[0]), peak, total)
        if d:
            send_part(0, d)

    def mid_weigh(i, d_a, d_b):
        q = jnp.concatenate([mid_q[lax.rem(x + d, 4)] for d in (d_a, d_b)], axis=0)
        return weigh_tile(lambda j: mid[0, j], q, scores, weights.at[i])

    def mid_sum(i, d_a, d_b, peak, total):
        sums = sum_tile(lambda j: mid_vt[j], weights.at[i])
        for k, d in enumerate((d_a, d_b)):
            cut = slice(k * ROWS, (k + 1) * ROWS)
            pack(mid_part, d, sums[:, cut], peak[:, cut], total[:, cut])
            if d:
                send_part(1, d)

    z_start(0)
    z_start(1)
    z_start(2)
    own_queries()
    own_block(0)
    own_block(1)
    relay_block(2)
    relay_block(3)
    spread_block(0)
    m_start(0)
    m_start(1)
    spread_block(1)
    spread_queries()
    relay_block(0)
    relay_block(1)
    wait_block(0)
    wait_block(1)
    turn_values(0, full_vt)
    wait_queries(0)
    full_tile(2)
    spread_block(4)
    full_tile(1)
    spread_block(5)
    full_tile(3)
    full_tile(0)
    relay_block(4)
    relay_block(5)
    own_landed()
    wait_queries(1)
    wait_block(2)
    wait_block(3)
    wait_block(4)
    first_pair = mid_weigh(0, 2, 1)
    other_pair = mid_weigh(1, 3, 0)
    wait_block(5)
    turn_values(1, mid_vt)
    mid_sum(0, 2, 1, *first_pair)
    mid_sum(1, 3, 0, *other_pair)
    z_sent(0)
    z_sent(1)
    z_sent(2)
    m_sent(0)
    m_sent(1)

    r = role(z)
    first = lax.rem(z + 12, 16) // 8
    head_base = lax.rem(z + 4, 8) * 3

    def hand_over(out, row, head, tz, sem):
        src = out.at[pl.ds(pl.multiple_of(row, OUT_ROWS), OUT_ROWS)]
        dst = landed.at[:, pl.ds(pl.multiple_of(head * HD, HD), HD)]
        return src, dst, sem, o_r, (((x * 4 + y) * 2 + tz // 8) * 2 + c, lax.rem(tz, 8))

    landed_all(full_got, p_r.at[0])
    full_out[...] = merge([full_part[0]] + [full_got[i] for i in range(3)])
    for d in range(16):
        tz = lax.rem(z + d, 16)
        s = lax.rem(first + tz // 8, 2)
        move = hand_over(full_out, s * ROWS + lax.rem(tz, 8) * OUT_ROWS, head_base + 2 * r, tz, o_s.at[0])
        if d:
            send(*move)
        else:
            pltpu.make_async_copy(move[0], move[1], o_r).start()

    landed_all(mid_got, p_r.at[1])
    mid_out[...] = merge([mid_part[0]] + [mid_got[i] for i in range(3)])
    for d in range(8):
        tl = lax.rem(zl + d, 8)
        move = hand_over(mid_out, tl * OUT_ROWS, zl * 3 + 1, z - zl + tl, o_s.at[1])
        if d:
            send(*move)
        else:
            pltpu.make_async_copy(move[0], move[1], o_r).start()

    landed_all(landed, o_r)
    o_ref[...] = landed[...]
    landed_all(full.at[:, pl.ds(0, 6)], y_s)
    landed_all(full, c_s)
    landed_all(full.at[0, :, pl.ds(0, 144)], x_s)
    landed_all(full_got, p_s.at[0])
    landed_all(mid_got, p_s.at[1])
    landed_all(landed.at[:, pl.ds(0, 15 * HD)], o_s.at[0])

    landed_all(landed.at[:, pl.ds(0, 7 * HD)], o_s.at[1])


def on_device(query_rows, key_rows, value_rows):
    dma = pltpu.SemaphoreType.DMA
    return pl.pallas_call(
        kernel,
        out_shape=pltpu.VMEM((OUT_ROWS, 24 * HD), BF16),
        in_specs=[pl.BlockSpec(memory_space=pl.ANY)] * 3,
        out_specs=pl.BlockSpec(memory_space=pltpu.VMEM),
        scratch_shapes=[
            pltpu.VMEM((2, 8, 256, HD), BF16),
            pltpu.VMEM((2, 8, 256, HD), BF16),
            pltpu.VMEM((4, 256, HD), BF16),
            pltpu.VMEM((4, 128, HD), BF16),
            pltpu.VMEM((8, HD, 256), BF16),
            pltpu.VMEM((8, HD, 256), BF16),
            pltpu.VMEM((8, 256, 256), F32),
            pltpu.VMEM((2, 8, 256, 256), BF16),
            pltpu.VMEM((4, HD + 8, 256), F32),
            pltpu.VMEM((4, HD + 8, 128), F32),
            pltpu.VMEM((3, HD + 8, 256), F32),
            pltpu.VMEM((3, HD + 8, 128), F32),
            pltpu.VMEM((256, HD), BF16),
            pltpu.VMEM((128, HD), BF16),
            pltpu.VMEM((OUT_ROWS, 24 * HD), BF16),
            dma((5,)), dma((5,)),
            dma(()), dma((6, 3)),
            dma(()), dma((6,)),
            dma(()), dma((2,)),
            dma((2,)), dma((2,)),
            dma((2,)), dma(()), dma(()),
        ],
        compiler_params=pltpu.CompilerParams(
            collective_id=0, has_side_effects=True, vmem_limit_bytes=60 * 2**20
        ),
        name="attend",
    )(query_rows, key_rows, value_rows)


def solution(mesh):
    return jax.shard_map(
        on_device,
        mesh=mesh,
        in_specs=(P("blk", "ulysses"), P("blk", "ulysses"), P("blk", "ulysses")),
        out_specs=P(("blk", "ulysses"), None),
        check_vma=False,
    )
```

```python
import functools

import jax
import jax.numpy as jnp
from jax import lax
from jax.experimental import pallas as pl
from jax.experimental.pallas import tpu as pltpu
from jax.sharding import PartitionSpec as P

HD = 128
ROWS = 128
OUT_ROWS = 16
MESH = pl.DeviceIdType.MESH
FACTOR = HD**-0.5 * 1.4426950408889634
F32 = jnp.float32
BF16 = jnp.bfloat16


def role(z):
    return 1 - lax.rem((z + 4) // 8, 2)


def weigh_tile(keys_at, q, scores, weights):
    peak = jnp.full((8, q.shape[0]), -jnp.inf, F32)
    for j in range(8):
        s = lax.dot_general(keys_at(j), q, (((1,), (1,)), ((), ())), preferred_element_type=F32)
        scores[j] = s
        peak = jnp.maximum(peak, jnp.max(s.reshape(32, 8, -1), axis=0))
    peak = jnp.max(peak, axis=0, keepdims=True)
    total = jnp.zeros((8, q.shape[0]), F32)
    for j in range(8):
        p = jnp.exp2((scores[j] - peak) * FACTOR)
        total = total + jnp.sum(p.reshape(32, 8, -1), axis=0)
        weights[j] = p.astype(BF16)
    return peak, jnp.sum(total, axis=0, keepdims=True)


def sum_tile(values_at, weights):
    return sum(jnp.dot(values_at(j), weights[j], preferred_element_type=F32) for j in range(8))


def pack(ref, at, sums, peak, total):
    ref[at, :HD] = sums
    ref[at, HD:] = jnp.concatenate([peak, total, jnp.zeros((6, peak.shape[1]), F32)], axis=0)


def merge(parts):
    peaks = [p[HD : HD + 1] for p in parts]
    top = functools.reduce(jnp.maximum, peaks)
    fades = [jnp.exp2((peak - top) * FACTOR) for peak in peaks]
    total = sum(p[HD + 1 : HD + 2] * f for p, f in zip(parts, fades))
    sums = sum(p[:HD] * f for p, f in zip(parts, fades))
    return (sums / total).T.astype(BF16)


def kernel(
    q_ref, k_ref, v_ref, o_ref,
    full, mid, full_q, mid_q, full_vt, mid_vt, scores, weights,
    full_part, mid_part, full_got, mid_got, full_out, mid_out, landed,
    z_s, z_r, y_s, y_r, c_s, c_r, x_s, x_r, p_s, p_r, o_s, o_r, l_s, met,
):
    b = lax.axis_index("blk")
    zl = lax.axis_index("ulysses")
    c = lax.rem(b, 2)
    z = lax.rem(b // 2, 2) * 8 + zl
    y = lax.rem(b // 4, 4)
    x = b // 16

    def at(dx=0, dy=0, dz=0, dc=0):
        tx, ty = lax.rem(x + dx, 4), lax.rem(y + dy, 4)
        tz, tc = lax.rem(z + dz, 16), lax.rem(c + dc, 2)
        return (((tx * 4 + ty) * 2 + tz // 8) * 2 + tc, lax.rem(tz, 8))

    def copy(src, dst, s_sem, r_sem, where):
        return pltpu.make_async_remote_copy(
            src_ref=src, dst_ref=dst, send_sem=s_sem, recv_sem=r_sem, device_id=where, device_id_type=MESH
        )

    def send(*args):
        copy(*args).start()

    def landed_all(ref, sem):
        pltpu.make_async_copy(ref, ref, sem).wait()

    barrier = pltpu.get_barrier_semaphore()
    peers = [at(dz=d) for d in (1, 2, 4, 12, 14, 15)]
    peers += [at(dy=d) for d in range(1, 4)] + [at(dx=d) for d in range(1, 4)] + [at(dc=1)]
    for peer in peers:
        pl.semaphore_signal(barrier, inc=1, device_id=peer, device_id_type=MESH)
    pl.semaphore_wait(barrier, len(peers))

    for d in (4, 12):
        pl.semaphore_signal(met, inc=1, device_id=at(dz=d), device_id_type=MESH)

    held_by, queries_by = (full, mid), (full_q, mid_q)
    columns = pl.ds(HD, HD)

    def block(head, kv, d, s=None):
        ref = held_by[head].at[kv, c * 4 + lax.rem(y - d + 4, 4)]
        return ref if s is None else ref.at[pl.ds(s * ROWS, ROWS)]

    def z_start(item):
        for s, dz in ((0, 4), (1, 12)):
            r = role(lax.rem(z + dz, 16))
            src = (k_ref, v_ref, q_ref)[item].at[:, pl.ds(pl.multiple_of(r * 256, 128), HD)]
            dst = full_q.at[x, pl.ds(s * ROWS, ROWS)] if item == 2 else block(0, item, 0, s)
            send(src, dst, z_s.at[item], z_r.at[item], at(dz=dz))

    def z_ref(item):
        return full_q.at[x] if item == 2 else block(0, item, 0)

    def z_sent(item):
        landed_all(z_ref(item), z_s.at[item])

    def m_start(kv):
        src = (k_ref, v_ref)[kv].at[:, columns]
        send(src, block(1, kv, 0, 1), z_s.at[3 + kv], z_r.at[3 + kv], at(dz=8))

    def m_sent(kv):
        landed_all(block(1, kv, 0, 1), z_s.at[3 + kv])

    def own_queries():
        src, dst = q_ref.at[:, columns], mid_q.at[x]
        for d in range(1, 4):
            send(src, dst, x_s, x_r.at[1], at(dx=d))
        pltpu.make_async_copy(src, dst, l_s).start()

    def own_block(kv):
        src, dst = (k_ref, v_ref)[kv].at[:, columns], block(1, kv, 0, 0)
        for d in range(1, 4):
            send(src, dst, y_s, y_r.at[2 + kv, d - 1], at(dy=d))
        send(src, dst, c_s, c_r.at[2 + kv], at(dc=1))
        pltpu.make_async_copy(src, dst, l_s).start()

    def own_landed():
        landed_all(mid.at[0, pl.ds(0, 3), pl.ds(0, ROWS)], l_s)

    def spread_queries():
        landed_all(z_ref(2), z_r.at[2])
        for d in range(1, 4):
            send(full_q.at[x], full_q.at[x], x_s, x_r.at[0], at(dx=d))

    def wait_queries(head):
        landed_all(queries_by[head].at[pl.ds(0, 3)], x_r.at[head])

    def kind_block(kind, d):
        return block(0, kind, d) if kind < 2 else block(1, kind % 2, d, kind // 2 - 1)

    def pass_on(kind, d):
        part = kind_block(kind, d)
        send(part, part, c_s, c_r.at[kind], at(dc=1))

    def spread_block(kind):
        part = kind_block(kind, 0)
        landed_all(part, z_r.at[kind if kind < 2 else kind - 1])
        for d in range(1, 4):
            send(part, part, y_s, y_r.at[kind, d - 1], at(dy=d))
        pass_on(kind, 0)

    def relay_block(kind):
        for d in range(1, 4):
            landed_all(kind_block(kind, d), y_r.at[kind, d - 1])
            pass_on(kind, d)

    def wait_block(kind):
        other = pl.ds((1 - c) * 4, 4)
        if kind < 2:
            landed_all(full.at[kind, other], c_r.at[kind])
        else:
            landed_all(mid.at[kind % 2, other, pl.ds((kind // 2 - 1) * ROWS, ROWS)], c_r.at[kind])

    def turn_values(head, turned):
        for j in range(8):
            turned[j] = held_by[head][1, j].T

    parts = ((full_part.at[0], full_got.at[0]), (full_part.at[1], full_got.at[1]), (mid_part, mid_got))

    def weigh(group, i, pair):
        if group == 2:
            q = [mid_q[lax.rem(x + d, 4)] for d in pair]
        else:
            q = [full_q[lax.rem(x + d, 4), group * ROWS : (group + 1) * ROWS] for d in pair]
        keys = mid if group == 2 else full
        return weigh_tile(lambda j: keys[0, j], jnp.concatenate(q, axis=0), scores, weights.at[i])

    def add_up(group, i, pair, weighed):
        turned = mid_vt if group == 2 else full_vt
        sums = sum_tile(lambda j: turned[j], weights.at[i])
        for k, d in enumerate(pair):
            cut = slice(k * ROWS, (k + 1) * ROWS)
            part, got = parts[group]
            pack(part, d, sums[:, cut], weighed[0][:, cut], weighed[1][:, cut])
            if d:
                send(part.at[d], got.at[d - 1], p_s.at[group], p_r.at[group], at(dx=d))

    def both(group, i, pair):
        add_up(group, i, pair, weigh(group, i, pair))

    z_start(0)
    z_start(1)
    z_start(2)
    own_queries()
    own_block(0)
    own_block(1)
    pl.semaphore_wait(met, 2)
    relay_block(2)
    relay_block(3)
    spread_block(0)
    m_start(0)
    m_start(1)
    spread_block(1)
    spread_queries()
    relay_block(0)
    relay_block(1)
    spread_block(4)
    wait_block(0)
    wait_block(1)
    turn_values(0, full_vt)
    wait_queries(0)
    both(0, 0, (2, 1))
    spread_block(5)
    both(0, 1, (3, 0))
    both(1, 0, (2, 1))
    relay_block(4)
    both(1, 1, (3, 0))
    relay_block(5)
    own_landed()
    wait_queries(1)
    wait_block(2)
    wait_block(3)
    wait_block(4)
    first_pair = weigh(2, 0, (2, 1))
    other_pair = weigh(2, 1, (3, 0))
    wait_block(5)
    turn_values(1, mid_vt)
    add_up(2, 0, (2, 1), first_pair)
    add_up(2, 1, (3, 0), other_pair)
    z_sent(0)
    z_sent(1)
    z_sent(2)
    m_sent(0)
    m_sent(1)

    r = role(z)
    first = lax.rem(z + 12, 16) // 8
    head_base = lax.rem(z + 4, 8) * 3

    def hand_over(out, row, head, tz, sem):
        src = out.at[pl.ds(pl.multiple_of(row, OUT_ROWS), OUT_ROWS)]
        dst = landed.at[:, pl.ds(pl.multiple_of(head * HD, HD), HD)]
        return src, dst, sem, o_r, (((x * 4 + y) * 2 + tz // 8) * 2 + c, lax.rem(tz, 8))

    for s in range(2):
        landed_all(full_got.at[s], p_r.at[s])
        full_out[s * ROWS : (s + 1) * ROWS] = merge([full_part[s, 0]] + [full_got[s, i] for i in range(3)])
        half = lax.rem(first + s, 2)
        for d in range(8):
            tl = lax.rem(zl + d, 8)
            move = hand_over(full_out, s * ROWS + tl * OUT_ROWS, head_base + 2 * r, half * 8 + tl, o_s.at[0])
            if d:
                send(*move)
                continue

            @pl.when(half != z // 8)
            def _():
                send(*move)

            @pl.when(half == z // 8)
            def _():
                pltpu.make_async_copy(move[0], move[1], o_r).start()

    landed_all(mid_got, p_r.at[2])
    mid_out[...] = merge([mid_part[0]] + [mid_got[i] for i in range(3)])
    for d in range(8):
        tl = lax.rem(zl + d, 8)
        move = hand_over(mid_out, tl * OUT_ROWS, zl * 3 + 1, z - zl + tl, o_s.at[1])
        if d:
            send(*move)
        else:
            pltpu.make_async_copy(move[0], move[1], o_r).start()

    landed_all(landed, o_r)
    o_ref[...] = landed[...]
    landed_all(full.at[:, pl.ds(0, 6)], y_s)
    landed_all(full, c_s)
    landed_all(full.at[0, :, pl.ds(0, 144)], x_s)
    landed_all(full_got.at[0], p_s.at[0])
    landed_all(full_got.at[1], p_s.at[1])
    landed_all(mid_got, p_s.at[2])
    landed_all(landed.at[:, pl.ds(0, 15 * HD)], o_s.at[0])

    landed_all(landed.at[:, pl.ds(0, 7 * HD)], o_s.at[1])


def on_device(query_rows, key_rows, value_rows):
    dma = pltpu.SemaphoreType.DMA
    return pl.pallas_call(
        kernel,
        out_shape=pltpu.VMEM((OUT_ROWS, 24 * HD), BF16),
        in_specs=[pl.BlockSpec(memory_space=pl.ANY)] * 3,
        out_specs=pl.BlockSpec(memory_space=pltpu.VMEM),
        scratch_shapes=[
            pltpu.VMEM((2, 8, 256, HD), BF16),
            pltpu.VMEM((2, 8, 256, HD), BF16),
            pltpu.VMEM((4, 256, HD), BF16),
            pltpu.VMEM((4, 128, HD), BF16),
            pltpu.VMEM((8, HD, 256), BF16),
            pltpu.VMEM((8, HD, 256), BF16),
            pltpu.VMEM((8, 256, 256), F32),
            pltpu.VMEM((2, 8, 256, 256), BF16),
            pltpu.VMEM((2, 4, HD + 8, 128), F32),
            pltpu.VMEM((4, HD + 8, 128), F32),
            pltpu.VMEM((2, 3, HD + 8, 128), F32),
            pltpu.VMEM((3, HD + 8, 128), F32),
            pltpu.VMEM((256, HD), BF16),
            pltpu.VMEM((128, HD), BF16),
            pltpu.VMEM((OUT_ROWS, 24 * HD), BF16),
            dma((5,)), dma((5,)),
            dma(()), dma((6, 3)),
            dma(()), dma((6,)),
            dma(()), dma((2,)),
            dma((3,)), dma((3,)),
            dma((2,)), dma(()), dma(()), pltpu.SemaphoreType.REGULAR,
        ],
        compiler_params=pltpu.CompilerParams(
            collective_id=0, has_side_effects=True, vmem_limit_bytes=60 * 2**20
        ),
        name="attend",
    )(query_rows, key_rows, value_rows)


def solution(mesh):
    return jax.shard_map(
        on_device,
        mesh=mesh,
        in_specs=(P("blk", "ulysses"), P("blk", "ulysses"), P("blk", "ulysses")),
        out_specs=P(("blk", "ulysses"), None),
        check_vma=False,
    )
```

```python
import functools

import jax
import jax.numpy as jnp
from jax import lax
from jax.experimental import pallas as pl
from jax.experimental.pallas import tpu as pltpu
from jax.sharding import PartitionSpec as P

HD = 128
ROWS = 128
OUT_ROWS = 16
MESH = pl.DeviceIdType.MESH
FACTOR = HD**-0.5 * 1.4426950408889634
F32 = jnp.float32
BF16 = jnp.bfloat16


def role(z):
    return 1 - lax.rem((z + 4) // 8, 2)


def weigh_tile(keys_at, q, scores, weights):
    peak = jnp.full((8, q.shape[0]), -jnp.inf, F32)
    for j in range(8):
        s = lax.dot_general(keys_at(j), q, (((1,), (1,)), ((), ())), preferred_element_type=F32)
        scores[j] = s
        peak = jnp.maximum(peak, jnp.max(s.reshape(32, 8, -1), axis=0))
    peak = jnp.max(peak, axis=0, keepdims=True)
    total = jnp.zeros((8, q.shape[0]), F32)
    for j in range(8):
        p = jnp.exp2((scores[j] - peak) * FACTOR)
        total = total + jnp.sum(p.reshape(32, 8, -1), axis=0)
        weights[j] = p.astype(BF16)
    return peak, jnp.sum(total, axis=0, keepdims=True)


def sum_tile(values_at, weights):
    return sum(jnp.dot(values_at(j), weights[j], preferred_element_type=F32) for j in range(8))


def pack(ref, at, sums, peak, total):
    ref[at, :HD] = sums
    ref[at, HD:] = jnp.concatenate([peak, total, jnp.zeros((6, peak.shape[1]), F32)], axis=0)


def merge(parts):
    peaks = [p[HD : HD + 1] for p in parts]
    top = functools.reduce(jnp.maximum, peaks)
    fades = [jnp.exp2((peak - top) * FACTOR) for peak in peaks]
    total = sum(p[HD + 1 : HD + 2] * f for p, f in zip(parts, fades))
    sums = sum(p[:HD] * f for p, f in zip(parts, fades))
    return (sums / total).T.astype(BF16)


def kernel(
    q_ref, k_ref, v_ref, o_ref,
    full, mid, full_q, mid_q, full_vt, mid_vt, scores, weights,
    full_part, mid_part, full_got, mid_got, full_out, mid_out, landed,
    z_s, z_r, y_s, y_r, c_s, c_r, x_s, x_r, p_s, p_r, o_s, o_r, l_s, met,
):
    b = lax.axis_index("blk")
    zl = lax.axis_index("ulysses")
    c = lax.rem(b, 2)
    z = lax.rem(b // 2, 2) * 8 + zl
    y = lax.rem(b // 4, 4)
    x = b // 16

    def at(dx=0, dy=0, dz=0, dc=0):
        tx, ty = lax.rem(x + dx, 4), lax.rem(y + dy, 4)
        tz, tc = lax.rem(z + dz, 16), lax.rem(c + dc, 2)
        return (((tx * 4 + ty) * 2 + tz // 8) * 2 + tc, lax.rem(tz, 8))

    def copy(src, dst, s_sem, r_sem, where):
        return pltpu.make_async_remote_copy(
            src_ref=src, dst_ref=dst, send_sem=s_sem, recv_sem=r_sem, device_id=where, device_id_type=MESH
        )

    def send(*args):
        copy(*args).start()

    def landed_all(ref, sem):
        pltpu.make_async_copy(ref, ref, sem).wait()

    barrier = pltpu.get_barrier_semaphore()
    peers = [at(dz=d) for d in (1, 2, 4, 12, 14, 15)]
    peers += [at(dy=d) for d in range(1, 4)] + [at(dx=d) for d in range(1, 4)] + [at(dc=1)]
    for peer in peers:
        pl.semaphore_signal(barrier, inc=1, device_id=peer, device_id_type=MESH)
    pl.semaphore_wait(barrier, len(peers))

    for d in (4, 12):
        pl.semaphore_signal(met, inc=1, device_id=at(dz=d), device_id_type=MESH)

    held_by, queries_by = (full, mid), (full_q, mid_q)
    columns = pl.ds(HD, HD)

    def block(head, kv, d, s=None):
        ref = held_by[head].at[kv, c * 4 + lax.rem(y - d + 4, 4)]
        return ref if s is None else ref.at[pl.ds(s * ROWS, ROWS)]

    def z_start(item):
        for s, dz in ((0, 4), (1, 12)):
            r = role(lax.rem(z + dz, 16))
            src = (k_ref, v_ref, q_ref)[item].at[:, pl.ds(pl.multiple_of(r * 256, 128), HD)]
            dst = full_q.at[x, pl.ds(s * ROWS, ROWS)] if item == 2 else block(0, item, 0, s)
            send(src, dst, z_s.at[item], z_r.at[item], at(dz=dz))

    def z_ref(item):
        return full_q.at[x] if item == 2 else block(0, item, 0)

    def z_sent(item):
        landed_all(z_ref(item), z_s.at[item])

    def m_start(kv):
        src = (k_ref, v_ref)[kv].at[:, columns]
        send(src, block(1, kv, 0, 1), z_s.at[3 + kv], z_r.at[3 + kv], at(dz=8))

    def m_sent(kv):
        landed_all(block(1, kv, 0, 1), z_s.at[3 + kv])

    def own_queries():
        src, dst = q_ref.at[:, columns], mid_q.at[x]
        for d in range(1, 4):
            send(src, dst, x_s, x_r.at[1], at(dx=d))
        pltpu.make_async_copy(src, dst, l_s).start()

    def own_block(kv):
        src, dst = (k_ref, v_ref)[kv].at[:, columns], block(1, kv, 0, 0)
        for d in range(1, 4):
            send(src, dst, y_s, y_r.at[2 + kv, d - 1], at(dy=d))
        send(src, dst, c_s, c_r.at[2 + kv], at(dc=1))
        pltpu.make_async_copy(src, dst, l_s).start()

    def own_landed():
        landed_all(mid.at[0, pl.ds(0, 3), pl.ds(0, ROWS)], l_s)

    def spread_queries():
        landed_all(z_ref(2), z_r.at[2])
        for d in range(1, 4):
            send(full_q.at[x], full_q.at[x], x_s, x_r.at[0], at(dx=d))

    def wait_queries(head):
        landed_all(queries_by[head].at[pl.ds(0, 3)], x_r.at[head])

    def kind_block(kind, d):
        return block(0, kind, d) if kind < 2 else block(1, kind % 2, d, kind // 2 - 1)

    def pass_on(kind, d):
        part = kind_block(kind, d)
        send(part, part, c_s, c_r.at[kind], at(dc=1))

    def spread_block(kind):
        part = kind_block(kind, 0)
        landed_all(part, z_r.at[kind if kind < 2 else kind - 1])
        for d in range(1, 4):
            send(part, part, y_s, y_r.at[kind, d - 1], at(dy=d))
        pass_on(kind, 0)

    def relay_block(kind):
        for d in range(1, 4):
            landed_all(kind_block(kind, d), y_r.at[kind, d - 1])
            pass_on(kind, d)

    def wait_block(kind):
        other = pl.ds((1 - c) * 4, 4)
        if kind < 2:
            landed_all(full.at[kind, other], c_r.at[kind])
        else:
            landed_all(mid.at[kind % 2, other, pl.ds((kind // 2 - 1) * ROWS, ROWS)], c_r.at[kind])

    def turn_values(head, turned):
        for j in range(8):
            turned[j] = held_by[head][1, j].T

    parts = ((full_part.at[0], full_got.at[0]), (full_part.at[1], full_got.at[1]), (mid_part, mid_got))

    def weigh(group, i, pair):
        if group == 2:
            q = [mid_q[lax.rem(x + d, 4)] for d in pair]
        else:
            q = [full_q[lax.rem(x + d, 4), group * ROWS : (group + 1) * ROWS] for d in pair]
        keys = mid if group == 2 else full
        return weigh_tile(lambda j: keys[0, j], jnp.concatenate(q, axis=0), scores, weights.at[i])

    def add_up(group, i, pair, weighed):
        turned = mid_vt if group == 2 else full_vt
        sums = sum_tile(lambda j: turned[j], weights.at[i])
        for k, d in enumerate(pair):
            cut = slice(k * ROWS, (k + 1) * ROWS)
            part, got = parts[group]
            pack(part, d, sums[:, cut], weighed[0][:, cut], weighed[1][:, cut])
            if d:
                send(part.at[d], got.at[d - 1], p_s.at[group], p_r.at[group], at(dx=d))

    def both(group, i, pair):
        add_up(group, i, pair, weigh(group, i, pair))

    z_start(0)
    z_start(1)
    z_start(2)
    own_queries()
    own_block(0)
    own_block(1)
    pl.semaphore_wait(met, 2)
    relay_block(2)
    relay_block(3)
    spread_block(0)
    m_start(0)
    m_start(1)
    spread_queries()
    spread_block(1)
    relay_block(0)
    relay_block(1)
    spread_block(4)
    wait_block(0)
    wait_block(1)
    turn_values(0, full_vt)
    wait_queries(0)
    both(0, 0, (2, 1))
    spread_block(5)
    both(0, 1, (3, 0))
    both(1, 0, (2, 1))
    relay_block(4)
    both(1, 1, (3, 0))
    relay_block(5)
    own_landed()
    wait_queries(1)
    wait_block(2)
    wait_block(3)
    wait_block(4)
    first_pair = weigh(2, 0, (2, 1))
    other_pair = weigh(2, 1, (3, 0))
    wait_block(5)
    turn_values(1, mid_vt)
    add_up(2, 0, (2, 1), first_pair)
    add_up(2, 1, (3, 0), other_pair)
    z_sent(0)
    z_sent(1)
    z_sent(2)
    m_sent(0)
    m_sent(1)

    r = role(z)
    first = lax.rem(z + 12, 16) // 8
    head_base = lax.rem(z + 4, 8) * 3

    def hand_over(out, row, head, tz, sem):
        src = out.at[pl.ds(pl.multiple_of(row, OUT_ROWS), OUT_ROWS)]
        dst = landed.at[:, pl.ds(pl.multiple_of(head * HD, HD), HD)]
        return src, dst, sem, o_r, (((x * 4 + y) * 2 + tz // 8) * 2 + c, lax.rem(tz, 8))

    for s in range(2):
        landed_all(full_got.at[s], p_r.at[s])
        full_out[s * ROWS : (s + 1) * ROWS] = merge([full_part[s, 0]] + [full_got[s, i] for i in range(3)])
        half = lax.rem(first + s, 2)
        for d in range(8):
            tl = lax.rem(zl + d, 8)
            move = hand_over(full_out, s * ROWS + tl * OUT_ROWS, head_base + 2 * r, half * 8 + tl, o_s.at[0])
            if d:
                send(*move)
                continue

            @pl.when(half != z // 8)
            def _():
                send(*move)

            @pl.when(half == z // 8)
            def _():
                pltpu.make_async_copy(move[0], move[1], o_r).start()

    landed_all(mid_got, p_r.at[2])
    mid_out[...] = merge([mid_part[0]] + [mid_got[i] for i in range(3)])
    for d in range(8):
        tl = lax.rem(zl + d, 8)
        move = hand_over(mid_out, tl * OUT_ROWS, zl * 3 + 1, z - zl + tl, o_s.at[1])
        if d:
            send(*move)
        else:
            pltpu.make_async_copy(move[0], move[1], o_r).start()

    landed_all(landed, o_r)
    o_ref[...] = landed[...]
    landed_all(full.at[:, pl.ds(0, 6)], y_s)
    landed_all(full, c_s)
    landed_all(full.at[0, :, pl.ds(0, 144)], x_s)
    landed_all(full_got.at[0], p_s.at[0])
    landed_all(full_got.at[1], p_s.at[1])
    landed_all(mid_got, p_s.at[2])
    landed_all(landed.at[:, pl.ds(0, 15 * HD)], o_s.at[0])

    landed_all(landed.at[:, pl.ds(0, 7 * HD)], o_s.at[1])


def on_device(query_rows, key_rows, value_rows):
    dma = pltpu.SemaphoreType.DMA
    return pl.pallas_call(
        kernel,
        out_shape=pltpu.VMEM((OUT_ROWS, 24 * HD), BF16),
        in_specs=[pl.BlockSpec(memory_space=pl.ANY)] * 3,
        out_specs=pl.BlockSpec(memory_space=pltpu.VMEM),
        scratch_shapes=[
            pltpu.VMEM((2, 8, 256, HD), BF16),
            pltpu.VMEM((2, 8, 256, HD), BF16),
            pltpu.VMEM((4, 256, HD), BF16),
            pltpu.VMEM((4, 128, HD), BF16),
            pltpu.VMEM((8, HD, 256), BF16),
            pltpu.VMEM((8, HD, 256), BF16),
            pltpu.VMEM((8, 256, 256), F32),
            pltpu.VMEM((2, 8, 256, 256), BF16),
            pltpu.VMEM((2, 4, HD + 8, 128), F32),
            pltpu.VMEM((4, HD + 8, 128), F32),
            pltpu.VMEM((2, 3, HD + 8, 128), F32),
            pltpu.VMEM((3, HD + 8, 128), F32),
            pltpu.VMEM((256, HD), BF16),
            pltpu.VMEM((128, HD), BF16),
            pltpu.VMEM((OUT_ROWS, 24 * HD), BF16),
            dma((5,)), dma((5,)),
            dma(()), dma((6, 3)),
            dma(()), dma((6,)),
            dma(()), dma((2,)),
            dma((3,)), dma((3,)),
            dma((2,)), dma(()), dma(()), pltpu.SemaphoreType.REGULAR,
        ],
        compiler_params=pltpu.CompilerParams(
            collective_id=0, has_side_effects=True, vmem_limit_bytes=60 * 2**20
        ),
        name="attend",
    )(query_rows, key_rows, value_rows)


def solution(mesh):
    return jax.shard_map(
        on_device,
        mesh=mesh,
        in_specs=(P("blk", "ulysses"), P("blk", "ulysses"), P("blk", "ulysses")),
        out_specs=P(("blk", "ulysses"), None),
        check_vma=False,
    )
```
